32 devices in a mesh: bx: 8 (over z, x), by: 4 (over y, core).
Axes of the slice: x: 2, y: 2, z: 4, core: 2. Of those that a mesh axis runs over, the one named last changes fastest.
Arguments:
- features: float32 [8, 4, 128, 128], P('bx', 'by'), may hold values from -6 to 6
- send_list: int32 [8, 4, 4, 32], P('bx', 'by'), may hold values from 0 to 127, as said below
- pair_first: int32 [8, 4, 2048], P('bx', 'by'), may hold values from 0 to 127, as said below
- pair_second: int32 [8, 4, 2048], P('bx', 'by'), may hold values from 0 to 255, as said below
- pair_species: int32 [8, 4, 2048], P('bx', 'by'), may hold values from 0 to 15
- pair_vector: float32 [8, 4, 3, 2048], P('bx', 'by'), may hold values from -2.5 to 2.5
- live_pairs: int32 [8, 4], P('bx', 'by'), may hold values from 1024 to 2048, as said below
- force_target: float32 [8, 4, 3, 128], P('bx', 'by'), may hold values from -12 to 12
- w_a: float32 [128, 512], replicated, may hold values from -0.5 to 0.5
- w_b: float32 [128, 512], replicated, may hold values from -0.5 to 0.5
- w_radial: float32 [8, 512], replicated, may hold values from -6 to 6
- species_table: float32 [16, 512], replicated, may hold values from -3 to 3
- w_mid: float32 [512, 512], replicated, may hold values from -0.25 to 0.25
- w_out: float32 [512], replicated, may hold values from -0.25 to 0.25
Outputs:
- forces: float32 [8, 4, 3, 128], P('bx', 'by')
- grad_w_a: float32 [128, 512], replicated
- grad_w_b: float32 [128, 512], replicated
- grad_w_radial: float32 [8, 512], replicated
- grad_species_table: float32 [16, 512], replicated
- grad_w_mid: float32 [512, 512], replicated
- grad_w_out: float32 [512], replicated
The draws below stay inside these ranges and needn't reach their ends.
Inputs may be any that keep to these rules, and one draw needn't show every extreme that they name: `pair_first`: the first atom of a pair is a local atom of the brick. `pair_second`: below 128 a local atom other than the slot's first atom; 128 + d * 32 + g names ghost row g of direction d. `send_list`: for each brick and direction, 32 distinct local atoms. `live_pairs`: slots below it are live; in every draw some brick has all 2048 slots live.
All inputs are finite; a program needn't handle non-finite values.
Results may differ from the reference program's by a relative error of at most 0.0003.
Values sent between devices are 32-bit elements; how exact they have to be, the bound alone decides.
A program may use at most 64 MiB of HBM per device.

```python
import math
import jax
import jax.numpy as jnp
from jax import lax

F = 128
H = 512
NB = 8
NS = 16
ATOM_DEV = 128
PAIR_DEV = 2048
GHOST = 32
N_BX = 8
N_BY = 4


def pair_atoms(key):
    base = jax.random.fold_in(key, 101)
    k_first, k_coin, k_slot, k_step = jax.random.split(base, 4)
    shape = (N_BX, N_BY, PAIR_DEV)
    first = jax.random.randint(k_first, shape, 0, ATOM_DEV)
    coin = jax.random.randint(k_coin, shape, 0, 2)
    slot = jax.random.randint(k_slot, shape, 0, 4 * GHOST)
    offset = jax.random.randint(k_step, shape, 1, ATOM_DEV)
    second = jnp.where(coin == 1, ATOM_DEV + slot, (first + offset) % ATOM_DEV)
    return (first.astype(jnp.int32), second.astype(jnp.int32))


def draw_pair_first(key, part):
    return pair_atoms(key)[0]


def draw_pair_second(key, part):
    return pair_atoms(key)[1]


def draw_send_list(key, part):
    scores = jax.random.randint(jax.random.fold_in(key, 202), (N_BX, N_BY, 4, ATOM_DEV), 0, 1 << 20)
    scores = scores * ATOM_DEV + jnp.arange(ATOM_DEV, dtype=jnp.int32)
    picked = jnp.argsort(scores, axis=-1, stable=True)[..., :GHOST]
    return picked.astype(jnp.int32)


def draw_live_pairs(key, part):
    k_count, k_pick = jax.random.split(jax.random.fold_in(key, 303))
    bricks = N_BX * N_BY
    counts = jax.random.randint(k_count, (bricks,), PAIR_DEV // 2, PAIR_DEV + 1)
    pick = jax.random.randint(k_pick, (), 0, bricks)
    counts = jnp.where(jnp.arange(bricks) == pick, PAIR_DEV, counts)
    return counts.reshape(N_BX, N_BY).astype(jnp.int32)


def place_ends(values, own_key, low, largest):
    dims = values.shape
    index_at = [jax.random.randint(jax.random.fold_in(own_key, axis), (), 0, dims[axis]) for axis in range(len(dims))]
    values = values.at[tuple(index_at)].set(low)
    longest = dims.index(max(dims))
    index_at[longest] = (index_at[longest] + 1) % dims[longest]
    return values.at[tuple(index_at)].set(largest)


def steps_of(rng, dims, cuts, smallest, largest):
    gain, own = 1.0, jax.random.fold_in(rng, 6)
    for axis_at, blocks in cuts:
        steps = jnp.exp(jax.random.uniform(jax.random.fold_in(own, axis_at), (blocks,), jnp.float32, smallest / len(cuts), largest / len(cuts)))
        gain = gain * jnp.repeat(steps, dims[axis_at] // blocks).reshape([-1 if axis == axis_at else 1 for axis in range(len(dims))])
    return gain


def noise(key, shape, deviation, bound, cuts=(), kind=jnp.bfloat16):
    gain = steps_of(key, shape, cuts, -0.22, 0.18) if cuts else 1.0
    result = jax.random.normal(key, shape, jnp.float32) * deviation * gain
    return jnp.minimum(jnp.maximum(result, -bound), bound).astype(kind)


def setup_inputs(seed: int = 0) -> dict:
    arg_keys = jax.random.split(jax.random.key(seed), 15)
    features = noise(arg_keys[0], (N_BX, N_BY, ATOM_DEV, F), 1.0, 6.0, ((0, 8), (1, 4)), jnp.float32)
    send_list = draw_send_list(jax.random.fold_in(arg_keys[14], 71), 0)
    pair_first = draw_pair_first(jax.random.fold_in(arg_keys[14], 71), 0)
    pair_second = draw_pair_second(jax.random.fold_in(arg_keys[14], 71), 0)
    pair_species = place_ends(jax.random.randint(arg_keys[4], (N_BX, N_BY, PAIR_DEV), 0, NS), jax.random.fold_in(arg_keys[4], 1), 0, NS - 1).astype(jnp.int32)
    pair_vector = jnp.clip(jax.random.uniform(arg_keys[5], (N_BX, N_BY, 3, PAIR_DEV), jnp.float32, -2.5, 2.5) * steps_of(arg_keys[5], (N_BX, N_BY, 3, PAIR_DEV), ((0, 8), (1, 4)), -0.4, 0.0), -2.5, 2.5)
    live_pairs = draw_live_pairs(jax.random.fold_in(arg_keys[14], 71), 0)
    force_target = noise(arg_keys[7], (N_BX, N_BY, 3, ATOM_DEV), 2.0, 12.0, ((0, 8), (1, 4)), jnp.float32)
    w_a = noise(arg_keys[8], (F, H), F ** -0.5, 0.5, (), jnp.float32)
    w_b = noise(arg_keys[9], (F, H), F ** -0.5, 0.5, (), jnp.float32)
    w_radial = noise(arg_keys[10], (NB, H), 1.0, 6.0, (), jnp.float32)
    species_table = noise(arg_keys[11], (NS, H), 0.5, 3.0, (), jnp.float32)
    w_mid = noise(arg_keys[12], (H, H), H ** -0.5, 0.25, (), jnp.float32)
    w_out = noise(arg_keys[13], (H,), H ** -0.5, 0.25, (), jnp.float32)
    return {"features": features, "send_list": send_list, "pair_first": pair_first, "pair_second": pair_second, "pair_species": pair_species, "pair_vector": pair_vector, "live_pairs": live_pairs, "force_target": force_target, "w_a": w_a, "w_b": w_b, "w_radial": w_radial, "species_table": species_table, "w_mid": w_mid, "w_out": w_out}


DIRS = ((1, 0), (0, 1), (1, 1), (1, -1))
RCUT = 5.0

def pair_slope(params, first_rows, second_rows, kinds, vec):
    w_a, w_b, w_radial, species_table, w_mid, w_out = params
    highest = lax.Precision.HIGHEST
    square = lax.optimization_barrier(jnp.sum(vec * vec, axis=0)) + 1.0
    radius = jnp.sqrt(square)
    order = (jnp.arange(1, w_radial.shape[0] + 1).astype(vec.dtype) * (math.pi / RCUT))[:, None]
    phase = order * radius[None, :]
    basis = jnp.sin(phase) / radius
    basis_slope = order * jnp.cos(phase) / radius - jnp.sin(phase) / square
    pre = jnp.dot(first_rows, w_a, precision=highest) + jnp.dot(second_rows, w_b, precision=highest)
    pre = pre + jnp.dot(basis.T, w_radial, precision=highest) + jnp.dot(kinds, species_table, precision=highest)
    sig_pre = jax.nn.sigmoid(pre)
    mid = jnp.dot(pre * sig_pre, w_mid, precision=highest)
    sig_mid = jax.nn.sigmoid(mid)
    grad_mid = w_out * sig_mid * (1.0 + mid * (1.0 - sig_mid))
    grad_pre = jnp.dot(grad_mid, w_mid.T, precision=highest) * sig_pre * (1.0 + pre * (1.0 - sig_pre))
    along = jnp.dot(grad_pre, w_radial.T, precision=highest)
    return lax.optimization_barrier(jnp.sum(along.T * basis_slope, axis=0)) / radius

def ghost_rows(table, send_list):
    pieces = []
    for d, (dx, dy) in enumerate(DIRS):
        source = jnp.roll(table, (-dx, -dy), axis=(0, 1))
        chosen = jnp.roll(send_list[:, :, d, :], (-dx, -dy), axis=(0, 1))
        pieces.append(jnp.take_along_axis(source, chosen[..., None], axis=2))
    return jnp.concatenate(pieces, axis=2)

def reference(features, send_list, pair_first, pair_second, pair_species, pair_vector, live_pairs, force_target, w_a, w_b, w_radial, species_table, w_mid, w_out):
    highest = lax.Precision.HIGHEST
    nbx, nby, atoms, width = features.shape
    ghosts = send_list.shape[3]
    pairs = pair_first.shape[2]
    extent = atoms + 4 * ghosts
    params = (w_a, w_b, w_radial, species_table, w_mid, w_out)
    table = jnp.concatenate([features, ghost_rows(features, send_list)], axis=2)
    flat_table = table.reshape(nbx * nby, extent, width)
    flat_first = pair_first.reshape(nbx * nby, pairs)
    flat_second = pair_second.reshape(nbx * nby, pairs)
    flat_species = pair_species.reshape(nbx * nby, pairs)
    flat_vec = pair_vector.reshape(nbx * nby, 3, pairs)
    flat_live = live_pairs.reshape(nbx * nby)
    columns = jnp.arange(extent)
    kinds_all = jnp.arange(species_table.shape[0])

    def brick_inputs(rows, fi, se, sp, live):
        kinds = (sp[:, None] == kinds_all[None, :]).astype(jnp.float32)
        alive = jnp.arange(pairs) < live
        return (rows[fi], rows[se], kinds, alive)

    def brick_forces(args):
        rows, fi, se, sp, vec, live = args
        xi, xj, kinds, alive = brick_inputs(rows, fi, se, sp, live)
        coupling = jnp.where(alive, pair_slope(params, xi, xj, kinds, vec), 0.0)
        sign = (fi[:, None] == columns[None, :]).astype(jnp.float32) - (se[:, None] == columns[None, :]).astype(jnp.float32)
        return jnp.dot(coupling[None, :] * vec, sign, precision=highest)
    extended = lax.map(brick_forces, (flat_table, flat_first, flat_second, flat_species, flat_vec, flat_live))
    extended = extended.reshape(nbx, nby, 3, extent)
    forces = extended[..., :atoms]
    parts = extended[..., atoms:].reshape(nbx, nby, 3, 4, ghosts)
    atom_ids = jnp.arange(atoms)
    for d, (dx, dy) in enumerate(DIRS):
        arrived = jnp.roll(parts[:, :, :, d, :], (dx, dy), axis=(0, 1))
        onehot = (send_list[:, :, d, :, None] == atom_ids).astype(jnp.float32)
        forces = forces + jnp.einsum('xycg,xyga->xyca', arrived, onehot, precision=highest)
    residual = (forces - force_target) / atoms
    residual_rows = ghost_rows(jnp.transpose(residual, (0, 1, 3, 2)), send_list)
    residual_table = jnp.concatenate([residual, jnp.transpose(residual_rows, (0, 1, 3, 2))], axis=3)
    flat_residual = residual_table.reshape(nbx * nby, 3, extent)

    def brick_grads(carry, args):
        rows, fi, se, sp, vec, live, res = args
        xi, xj, kinds, alive = brick_inputs(rows, fi, se, sp, live)
        weight = jnp.where(alive, lax.optimization_barrier(jnp.sum((res[:, fi] - res[:, se]) * vec, axis=0)), 0.0)
        _, pull = jax.vjp(lambda p: pair_slope(p, xi, xj, kinds, vec), params)
        grads = pull(weight)[0]
        return (jax.tree.map(lambda a, b: a + b, carry, grads), None)
    zero = jax.tree.map(jnp.zeros_like, params)
    grads, _ = lax.scan(brick_grads, zero, (flat_table, flat_first, flat_second, flat_species, flat_vec, flat_live, flat_residual))
    return (forces, grads[0], grads[1], grads[2], grads[3], grads[4], grads[5])
```

```python
import functools
import math

import jax
import jax.numpy as jnp
from jax import lax
from jax.experimental import pallas as pl
from jax.experimental.pallas import tpu as pltpu
from jax.sharding import PartitionSpec as P

PBLOCK = 256
LANES = 128
RCUT = 5.0
CHUNK = 64
VMEM_BYTES = 56 * 1024 * 1024
MESH = pl.DeviceIdType.MESH
HIGHEST = lax.Precision.HIGHEST
F32 = jnp.float32
BF16 = jnp.bfloat16


def passed_along(block, axis, distance):
    devices = range(lax.axis_size(axis))
    route = [((i - distance) % len(devices), i) for i in devices]
    return lax.ppermute(block, axis, route)


def pull_x(value):
    return passed_along(value, "bx", -1)


def push_x(value):
    return passed_along(value, "bx", 1)


def pull_y(value):
    return passed_along(value, "by", -1)


def push_y(value):
    return passed_along(value, "by", 1)


def fetch_ghosts(rows):
    across = pull_x(jnp.stack([rows[0], rows[2], rows[3]]))
    upper = pull_y(jnp.stack([rows[1], across[1]]))
    lower = push_y(across[2])
    return jnp.stack([across[0], upper[0], upper[1], lower])


def return_partials(parts):
    upper = push_y(jnp.stack([parts[1], parts[2]]))
    lower = pull_y(parts[3])
    across = push_x(jnp.stack([parts[0], upper[1], lower]))
    return jnp.stack([across[0], upper[0], across[1], across[2]])


def split(x):
    hi = x.astype(BF16)
    return hi, (x - hi.astype(F32)).astype(BF16)


def mm(a, b):
    return jnp.dot(a, b, preferred_element_type=F32)


def mm_t(a, b):
    return lax.dot_general(a, b, (((1,), (1,)), ((), ())), preferred_element_type=F32)


def round_up(n, k):
    return -(-n // k) * k


def onehot(ids, rows, cols):
    return jnp.where(lax.broadcasted_iota(jnp.int32, (rows, cols), 0) == ids, 1.0, 0.0).astype(BF16)


def slopes_of(z):
    sig = 0.5 * jnp.tanh(0.5 * z) + 0.5
    rest = 1.0 - sig
    act = z * sig
    d1 = sig + act * rest
    d2 = sig * rest * (2.0 + z * rest - act)
    return act, d1, d2


def phase_one(
    atoms,
    live, first, second, species, vec, table, w_a, w_b, w_radial, species_table, w_mid, w_out,
    ext, m1, mt, u_hi, u_lo, eg, zt, xs,
    c_hi, c_lo, wt_hi, wt_lo, w_hi, w_lo, wo, za, ta, md, eg_hi, eg_lo, wide,
):
    step = pl.program_id(0)
    extent, width = table.shape
    hidden = w_mid.shape[0]
    nb, ns = w_radial.shape[0], species_table.shape[0]
    pb = first.shape[1]
    base = atoms + extent
    used = base + 2 * nb + ns

    @pl.when(step == 0)
    def _():
        wide[...] = jnp.zeros_like(wide)
        wide[0:atoms, :] = jnp.dot(table[0:atoms, :], w_a[...], precision=HIGHEST, preferred_element_type=F32)
        wide[atoms:base, :] = jnp.dot(table[...], w_b[...], precision=HIGHEST, preferred_element_type=F32)
        wide[base : base + nb, :] = w_radial[...]
        wide[base + nb : base + 2 * nb, :] = w_radial[...]
        wide[base + 2 * nb : used, :] = species_table[...]
        c_hi[...], c_lo[...] = split(wide[...].T)
        w_hi[...], w_lo[...] = split(w_mid[...])
        wt_hi[...], wt_lo[...] = split(w_mid[...].T)
        wo[...] = jnp.broadcast_to(w_out[...], (pb, hidden)).T
        ext[...] = jnp.zeros_like(ext)

    square = jnp.sum(vec[...] * vec[...], axis=0, keepdims=True) + 1.0
    radius = jnp.sqrt(square)
    order = (lax.broadcasted_iota(jnp.int32, (nb, pb), 0) + 1).astype(F32) * (math.pi / RCUT)
    phase = order * radius
    sine, cosine = jnp.sin(phase), jnp.cos(phase)
    basis = sine / radius
    slope_basis = (order * cosine / radius - sine / square) / radius
    basis_hi = basis.astype(BF16).astype(F32)
    slope_hi = slope_basis.astype(BF16).astype(F32)
    m1[0:atoms, :] = onehot(first[...], atoms, pb)
    m1[atoms:base, :] = onehot(second[...], extent, pb)
    m1[base : base + 2 * nb, :] = jnp.concatenate([basis_hi, basis - basis_hi], axis=0).astype(BF16)
    m1[base + 2 * nb : used, :] = onehot(species[...], ns, pb)
    m1[used:, :] = jnp.zeros((m1.shape[0] - used, pb), BF16)
    mt[0 : 2 * nb, :] = jnp.concatenate([slope_hi, slope_basis - slope_hi], axis=0).astype(BF16)
    mt[2 * nb :, :] = jnp.zeros((mt.shape[0] - 2 * nb, pb), BF16)

    za[...] = mm(c_hi[...], m1[...]) + mm(c_lo[...], m1[...])
    ta[...] = mm(c_hi[:, base:], mt[...]) + mm(c_lo[:, base:], mt[...])
    for i in range(0, hidden, CHUNK):
        rows = slice(i, i + CHUNK)
        z, t = za[rows, :], ta[rows, :]
        act, d1, d2 = slopes_of(z)
        za[rows, :] = d1
        ta[rows, :] = d2 * t
        u_hi[rows, 0:pb], u_lo[rows, 0:pb] = split(act)
        u_hi[rows, pb:], u_lo[rows, pb:] = split(d1 * t)
    md[...] = mm(wt_hi[...], u_hi[...]) + mm(wt_lo[...], u_hi[...]) + mm(wt_hi[...], u_lo[...])
    slope = jnp.zeros((1, pb), F32)
    for i in range(0, hidden, CHUNK):
        rows = slice(i, i + CHUNK)
        m, dm, out = md[rows, 0:pb], md[rows, pb:], wo[rows, :]
        _, d1, d2 = slopes_of(m)
        x = d1 * dm
        xs[rows, :] = x
        slope = slope + jnp.sum(out * x, axis=0, keepdims=True)
        e, g = out * d2 * dm, out * d1
        eg[rows, 0:pb] = e
        eg[rows, pb:] = g
        eg_hi[rows, 0:pb], eg_lo[rows, 0:pb] = split(e)
        eg_hi[rows, pb:], eg_lo[rows, pb:] = split(g)
    md[...] = mm(w_hi[...], eg_hi[...]) + mm(w_lo[...], eg_hi[...]) + mm(w_hi[...], eg_lo[...])
    for i in range(0, hidden, CHUNK):
        rows = slice(i, i + CHUNK)
        e, g, d1 = md[rows, 0:pb], md[rows, pb:], za[rows, :]
        zt[rows, 0:pb] = e * d1 + g * ta[rows, :]
        zt[rows, pb:] = g * d1
    slots = step * pb + lax.broadcasted_iota(jnp.int32, (1, pb), 1)
    coupling = jnp.where(slots < live[0, 0], slope, 0.0)
    pushed = coupling * vec[...]
    pushed_hi = pushed.astype(BF16).astype(F32)
    pushed2 = jnp.concatenate([pushed_hi, pushed - pushed_hi], axis=0).astype(BF16)
    half = pushed.shape[0]
    on_first = mm_t(pushed2, m1[0:atoms, :])
    on_second = mm_t(pushed2, m1[atoms:base, :])
    ext[:, 0:atoms] += on_first[0:half] + on_first[half:]
    ext[...] -= on_second[0:half] + on_second[half:]


def phase_two(
    atoms, nb, ns,
    live, first, vec, table, residual, m1, mt, u_hi, u_lo, eg, zt, xs,
    grads,
    we_hi, we_lo, zh, zl, th, tl, d_mid, d_wide, d_slope, d_out,
):
    step = pl.program_id(0)
    extent, width = table.shape
    hidden = u_hi.shape[0]
    pb = first.shape[1]
    base = atoms + extent

    @pl.when(step == 0)
    def _():
        d_mid[...] = jnp.zeros_like(d_mid)
        d_wide[...] = jnp.zeros_like(d_wide)
        d_slope[...] = jnp.zeros_like(d_slope)
        d_out[...] = jnp.zeros_like(d_out)

    res = residual[...]
    res_hi = res.astype(BF16).astype(F32)
    res2 = jnp.concatenate([res_hi, res - res_hi], axis=0).astype(BF16)
    half = res.shape[0]
    apart = mm(res2[:, 0:atoms], m1[0:atoms, :]) - mm(res2, m1[atoms:base, :])
    slots = step * pb + lax.broadcasted_iota(jnp.int32, (1, pb), 1)
    pulled = jnp.sum((apart[0:half] + apart[half:]) * vec[...], axis=0, keepdims=True)
    weight = jnp.where(slots < live[0, 0], pulled, 0.0)
    for i in range(0, hidden, CHUNK):
        rows = slice(i, i + CHUNK)
        we_hi[rows, 0:pb], we_lo[rows, 0:pb] = split(eg[rows, 0:pb] * weight)
        we_hi[rows, pb:], we_lo[rows, pb:] = split(eg[rows, pb:] * weight)
        zh[rows, :], zl[rows, :] = split(zt[rows, 0:pb] * weight)
        th[rows, :], tl[rows, :] = split(zt[rows, pb:] * weight)
        x = xs[rows, :] * weight
        total = d_out[rows, :]
        for j in range(0, pb, LANES):
            total = total + x[:, j : j + LANES]
        d_out[rows, :] = total
    d_mid[...] += mm_t(u_hi[...], we_hi[...]) + mm_t(u_lo[...], we_hi[...]) + mm_t(u_hi[...], we_lo[...])
    d_wide[...] += mm_t(m1[...], zh[...]) + mm_t(m1[...], zl[...])
    d_slope[...] += mm_t(mt[0 : 2 * nb, :], th[...]) + mm_t(mt[0 : 2 * nb, :], tl[...])

    @pl.when(step == pl.num_programs(0) - 1)
    def _():
        across = table[...].T
        d_a = jnp.dot(across[:, 0:atoms], d_wide[0:atoms, :], precision=HIGHEST, preferred_element_type=F32)
        d_b = jnp.dot(across, d_wide[atoms:base, :], precision=HIGHEST, preferred_element_type=F32)
        d_radial = (
            d_wide[base : base + nb, :] + d_wide[base + nb : base + 2 * nb, :]
            + d_slope[0:nb, :] + d_slope[nb:, :]
        )
        d_species = d_wide[base + 2 * nb : base + 2 * nb + ns, :]
        d_last = jnp.broadcast_to(jnp.sum(d_out[...].T, axis=0, keepdims=True), (8, hidden))
        at = 0
        for piece in (d_a, d_b, d_mid[...], d_species, d_radial, d_last):
            n = piece.shape[0]
            for j in range(grads.shape[0]):
                grads[j, at : at + n, :] = piece[:, j * LANES : (j + 1) * LANES]
            at += n
        if at < grads.shape[1]:
            grads[:, at:, :] = jnp.zeros((grads.shape[0], grads.shape[1] - at, LANES), F32)


def unpack(packed, *outs):
    at = 0
    for out in outs:
        n = out.shape[0]
        for j in range(packed.shape[0]):
            out[:, j * LANES : (j + 1) * LANES] = packed[j, at : at + n, :]
        at += n


def sum_kernel(sizes, cut, mine, out, acc, from_core, in_a, in_b, in_c, in_d, in_z, send, recv):
    gc, gx, gy, gz = sizes
    bx, by = lax.axis_index("bx"), lax.axis_index("by")
    c, y = lax.rem(by, gc), lax.div(by, gc)
    x, z = lax.rem(bx, gx), lax.div(bx, gx)

    def place(px, pz, py, pc):
        return (pz * gx + px, py * gc + pc)

    def peers(me, size):
        return [(k, lax.rem(me + k, size)) for k in range(1, size)]

    cores = [(k, p, place(x, z, y, p)) for k, p in peers(c, gc)]
    xs = [(k, p, place(p, z, y, c)) for k, p in peers(x, gx)]
    ys = [(k, p, place(x, z, p, c)) for k, p in peers(y, gy)]
    zs = [(k, p, place(x, p, y, c)) for k, p in peers(z, gz)]
    everyone = cores + xs + ys + zs
    barrier = pltpu.get_barrier_semaphore()
    for _, _, device in everyone:
        pl.semaphore_signal(barrier, inc=1, device_id=device, device_id_type=MESH)
    pl.semaphore_wait(barrier, len(everyone))
    count = [0]

    def go(src, dst, device):
        slot = count[0]
        count[0] += 1
        copy = pltpu.make_async_remote_copy(
            src_ref=src, dst_ref=dst, send_sem=send.at[slot], recv_sem=recv.at[slot],
            device_id=device, device_id_type=MESH,
        )
        copy.start()
        return copy

    def finish(copies):
        for copy in copies:
            copy.wait()

    lower, upper = pl.ds(0, cut), pl.ds(cut, acc.shape[3] - cut)
    finish([go(mine.at[p], from_core.at[k - 1], d) for k, p, d in cores])
    total = mine[c]
    for k in range(gc - 1):
        total = total + from_core[k]
    acc[...] = total
    first = [go(acc.at[p, :, :, lower], in_a.at[k - 1], d) for k, p, d in xs]
    other = [go(acc.at[:, p, :, upper], in_b.at[k - 1], d) for k, p, d in ys]
    finish(first)
    for k in range(gx - 1):
        acc[x, :, :, lower] += in_a[k]
    first = [go(acc.at[x, p, :, lower], in_c.at[k - 1], d) for k, p, d in ys]
    finish(other)
    for k in range(gy - 1):
        acc[:, y, :, upper] += in_b[k]
    other = [go(acc.at[p, y, :, upper], in_d.at[k - 1], d) for k, p, d in xs]
    finish(first)
    for k in range(gy - 1):
        acc[x, y, :, lower] += in_c[k]
    finish(other)
    for k in range(gx - 1):
        acc[x, y, :, upper] += in_d[k]
    finish([go(acc.at[x, y, p], in_z.at[k - 1], d) for k, p, d in zs])
    total = acc[x, y, z]
    for k in range(gz - 1):
        total = total + in_z[k]
    out[c, x, y, z] = total
    finish([go(out.at[c, x, y, z], out.at[c, x, y, z], d) for k, p, d in zs])
    here = out.at[c, x, y, :, lower]
    first = [go(here, here, d) for k, p, d in ys]
    here = out.at[c, x, y, :, upper]
    other = [go(here, here, d) for k, p, d in xs]
    finish(first)
    here = out.at[c, x, :, :, lower]
    first = [go(here, here, d) for k, p, d in xs]
    finish(other)
    here = out.at[c, :, y, :, upper]
    other = [go(here, here, d) for k, p, d in ys]
    finish(first)
    finish(other)
    finish([go(out.at[c], out.at[c], d) for k, p, d in cores])


def sum_everywhere(packed, sizes, rows):
    gc, gx, gy, gz = sizes
    cut = (rows // 8 + 1) // 2 * 8
    n_copies = 2 * (gc - 1) + 4 * (gx - 1) + 4 * (gy - 1) + 2 * (gz - 1)
    shape = (gc, gx, gy, gz, rows, LANES)

    def room(*dims):
        return pltpu.VMEM(tuple(max(d, 1) for d in dims) + (LANES,), F32)

    whole = pl.BlockSpec(memory_space=pltpu.VMEM)
    return pl.pallas_call(
        functools.partial(sum_kernel, sizes, cut),
        out_shape=jax.ShapeDtypeStruct(shape, F32),
        in_specs=[whole],
        out_specs=whole,
        scratch_shapes=[
            room(gx, gy, gz, rows),
            room(gc - 1, gx, gy, gz, rows),
            room(gx - 1, gy, gz, cut),
            room(gy - 1, gx, gz, rows - cut),
            room(gy - 1, gz, cut),
            room(gx - 1, gz, rows - cut),
            room(gz - 1, rows),
            pltpu.SemaphoreType.DMA((n_copies,)),
            pltpu.SemaphoreType.DMA((n_copies,)),
        ],
        compiler_params=pltpu.CompilerParams(
            collective_id=1, has_side_effects=True, vmem_limit_bytes=VMEM_BYTES
        ),
        name="sum_grads",
    )(packed.reshape(shape))


def local(
    features,
    send_list,
    pair_first,
    pair_second,
    pair_species,
    pair_vector,
    live_pairs,
    force_target,
    w_a,
    w_b,
    w_radial,
    species_table,
    w_mid,
    w_out,
):
    local_feat = features[0, 0]
    sends = send_list[0, 0]
    first, second, species = pair_first[0], pair_second[0], pair_species[0]
    vec = jnp.pad(pair_vector[0, 0], ((0, 5), (0, 0)))
    target = force_target[0, 0]
    atoms, width = local_feat.shape
    ghosts = sends.shape[1]
    extent = atoms + 4 * ghosts
    hidden = w_mid.shape[0]
    nb, ns = w_radial.shape[0], species_table.shape[0]
    pairs = first.shape[1]
    pb = min(PBLOCK, pairs)
    steps = pairs // pb
    deep = round_up(atoms + extent + 2 * nb + ns, LANES)
    thin = deep - atoms - extent

    lent = jnp.take(local_feat, sends, axis=0)
    arrived = fetch_ghosts(lent)
    table = jnp.concatenate([local_feat, arrived.reshape(4 * ghosts, width)], axis=0)

    smem = pl.BlockSpec(memory_space=pltpu.SMEM)

    def full(*dims):
        return pl.BlockSpec(dims, lambda i: (0,) * len(dims))

    def lane_block(rows):
        return pl.BlockSpec((rows, pb), lambda i: (0, i))

    def step_block(rows, cols):
        return pl.BlockSpec((None, rows, cols), lambda i: (i, 0, 0))

    def stacked(rows, cols, dtype):
        return jax.ShapeDtypeStruct((steps, rows, cols), dtype)

    params = pltpu.CompilerParams(
        dimension_semantics=("arbitrary",), vmem_limit_bytes=VMEM_BYTES
    )
    kept_specs = [
        step_block(deep, pb),
        step_block(thin, pb),
        step_block(hidden, 2 * pb),
        step_block(hidden, 2 * pb),
        step_block(hidden, 2 * pb),
        step_block(hidden, 2 * pb),
        step_block(hidden, pb),
    ]
    ext, *kept = pl.pallas_call(
        functools.partial(phase_one, atoms),
        grid=(steps,),
        out_shape=[
            jax.ShapeDtypeStruct((8, extent), F32),
            stacked(deep, pb, BF16),
            stacked(thin, pb, BF16),
            stacked(hidden, 2 * pb, BF16),
            stacked(hidden, 2 * pb, BF16),
            stacked(hidden, 2 * pb, F32),
            stacked(hidden, 2 * pb, F32),
            stacked(hidden, pb, F32),
        ],
        in_specs=[
            smem,
            lane_block(1),
            lane_block(1),
            lane_block(1),
            lane_block(8),
            full(extent, width),
            full(width, hidden),
            full(width, hidden),
            full(nb, hidden),
            full(ns, hidden),
            full(hidden, hidden),
            full(1, hidden),
        ],
        out_specs=[full(8, extent)] + kept_specs,
        scratch_shapes=[
            pltpu.VMEM((hidden, deep), BF16),
            pltpu.VMEM((hidden, deep), BF16),
            pltpu.VMEM((hidden, hidden), BF16),
            pltpu.VMEM((hidden, hidden), BF16),
            pltpu.VMEM((hidden, hidden), BF16),
            pltpu.VMEM((hidden, hidden), BF16),
            pltpu.VMEM((hidden, pb), F32),
            pltpu.VMEM((hidden, pb), F32),
            pltpu.VMEM((hidden, pb), F32),
            pltpu.VMEM((hidden, 2 * pb), F32),
            pltpu.VMEM((hidden, 2 * pb), BF16),
            pltpu.VMEM((hidden, 2 * pb), BF16),
            pltpu.VMEM((deep, hidden), F32),
        ],
        compiler_params=params,
        name="edge_forward",
    )(
        live_pairs, first, second, species, vec, table, w_a, w_b, w_radial, species_table, w_mid,
        w_out[None],
    )
    extended = ext[:3]
    parts = jnp.transpose(extended[:, atoms:].reshape(3, 4, ghosts), (1, 0, 2))
    returned = return_partials(parts)
    spots = (sends[:, :, None] == jnp.arange(atoms)[None, None, :]).astype(jnp.float32)
    forces = extended[:, :atoms] + jnp.einsum("dcg,dga->ca", returned, spots, precision=HIGHEST)
    residual = (forces - target) / atoms
    residual_lent = jnp.transpose(jnp.take(residual, sends, axis=1), (1, 0, 2))
    residual_ghosts = fetch_ghosts(residual_lent)
    residual_table = jnp.concatenate(
        [residual, jnp.transpose(residual_ghosts, (1, 0, 2)).reshape(3, 4 * ghosts)], axis=1
    )

    nbx, nby = lax.axis_size("bx"), lax.axis_size("by")
    gx = 2 if nbx % 2 == 0 else 1
    gc = 2 if nby % 2 == 0 else 1
    sizes = (gc, gx, nby // gc, nbx // gx)
    devices = nbx * nby
    columns = hidden // LANES
    body = 2 * width + hidden + ns + nb + 8
    rows = round_up(-(-body * columns // devices), 8)
    while devices * rows % (8 * columns):
        rows += 8
    tall = devices * rows // columns
    packed = pl.pallas_call(
        functools.partial(phase_two, atoms, nb, ns),
        grid=(steps,),
        out_shape=jax.ShapeDtypeStruct((columns, tall, LANES), F32),
        in_specs=[smem, lane_block(1), lane_block(8), full(extent, width), full(8, extent)]
        + kept_specs,
        out_specs=full(columns, tall, LANES),
        scratch_shapes=[
            pltpu.VMEM((hidden, 2 * pb), BF16),
            pltpu.VMEM((hidden, 2 * pb), BF16),
            pltpu.VMEM((hidden, pb), BF16),
            pltpu.VMEM((hidden, pb), BF16),
            pltpu.VMEM((hidden, pb), BF16),
            pltpu.VMEM((hidden, pb), BF16),
            pltpu.VMEM((hidden, hidden), F32),
            pltpu.VMEM((deep, hidden), F32),
            pltpu.VMEM((2 * nb, hidden), F32),
            pltpu.VMEM((hidden, LANES), F32),
        ],
        compiler_params=params,
        name="edge_backward",
    )(live_pairs, first, vec, table, jnp.pad(residual_table, ((0, 5), (0, 0))), *kept)
    summed = sum_everywhere(packed, sizes, rows).reshape(columns, tall, LANES)
    outs = pl.pallas_call(
        unpack,
        out_shape=[
            jax.ShapeDtypeStruct((n, hidden), F32) for n in (width, width, hidden, ns, nb, 8)
        ],
        compiler_params=pltpu.CompilerParams(vmem_limit_bytes=VMEM_BYTES),
        name="unpack_grads",
    )(summed)
    d_a, d_b, d_mid, d_species, d_radial, d_out = outs
    return (forces[None, None], d_a, d_b, d_radial, d_species, d_mid, d_out[0])


def solution(mesh):
    return jax.shard_map(
        local,
        mesh=mesh,
        in_specs=(
            P("bx", "by", None, None),
            P("bx", "by", None, None),
            P("bx", "by", None),
            P("bx", "by", None),
            P("bx", "by", None),
            P("bx", "by", None, None),
            P("bx", "by"),
            P("bx", "by", None, None),
            P(),
            P(),
            P(),
            P(),
            P(),
            P(),
        ),
        out_specs=(P("bx", "by", None, None), P(), P(), P(), P(), P(), P()),
        check_vma=False,
    )
```

```python
import functools
import math

import jax
import jax.numpy as jnp
from jax import lax
from jax.experimental import pallas as pl
from jax.experimental.pallas import tpu as pltpu
from jax.sharding import PartitionSpec as P

PBLOCK = 256
LANES = 128
RCUT = 5.0
CHUNK = 64
VMEM_BYTES = 56 * 1024 * 1024
MESH = pl.DeviceIdType.MESH
HIGHEST = lax.Precision.HIGHEST
F32 = jnp.float32
BF16 = jnp.bfloat16


DIRECTIONS = ((1, 0), (0, 1), (1, 1), (1, -1))


def greet():
    nbx, nby = lax.axis_size("bx"), lax.axis_size("by")
    bx, by = lax.axis_index("bx"), lax.axis_index("by")
    above = [(lax.rem(bx + dx, nbx), lax.rem(by + dy + nby, nby)) for dx, dy in DIRECTIONS]
    below = [(lax.rem(bx - dx + nbx, nbx), lax.rem(by - dy + nby, nby)) for dx, dy in DIRECTIONS]
    barrier = pltpu.get_barrier_semaphore()
    for device in above + below:
        pl.semaphore_signal(barrier, inc=1, device_id=device, device_id_type=MESH)
    pl.semaphore_wait(barrier, len(above + below))
    return above, below


def remote(src, dst, send, recv, device):
    copy = pltpu.make_async_remote_copy(
        src_ref=src, dst_ref=dst, send_sem=send, recv_sem=recv,
        device_id=device, device_id_type=MESH,
    )
    copy.start()
    return copy


def fetch_rows(features, sends, table, lent, send, recv):
    atoms = features.shape[0]
    ghosts = lent.shape[0] // len(DIRECTIONS)
    spots = lax.broadcasted_iota(jnp.int32, (atoms, lent.shape[0]), 0) == sends[...]
    spots = jnp.where(spots, 1.0, 0.0).T
    lent[...] = jnp.dot(spots, features[...], precision=HIGHEST, preferred_element_type=F32)
    table[0:atoms, :] = features[...]
    _, below = greet()
    copies = [
        remote(
            lent.at[pl.ds(d * ghosts, ghosts)], table.at[pl.ds(atoms + d * ghosts, ghosts)],
            send.at[d], recv.at[d], below[d],
        )
        for d in range(len(DIRECTIONS))
    ]
    for copy in copies:
        copy.wait()


def settle(ext, sends, target, forces, table, part, came, lent, back, send, recv):
    atoms = target.shape[1]
    count = part.shape[1]
    ghosts = count // len(DIRECTIONS)
    part[...] = ext[:, atoms:]
    above, below = greet()
    copies = [
        remote(part, came.at[d], send.at[d], recv.at[d], above[d]) for d in range(len(DIRECTIONS))
    ]
    spots = lax.broadcasted_iota(jnp.int32, (atoms, count), 0) == sends[...]
    spots = jnp.where(spots, 1.0, 0.0)
    lane = lax.broadcasted_iota(jnp.int32, part.shape, 1)

    def gathered(blocks):
        total = blocks[0]
        for d in range(1, len(DIRECTIONS)):
            total = jnp.where(lane >= d * ghosts, blocks[d], total)
        return total

    for copy in copies:
        copy.wait()
    returned = lax.dot_general(
        gathered(came), spots, (((1,), (1,)), ((), ())),
        precision=HIGHEST, preferred_element_type=F32,
    )
    force = ext[:, 0:atoms] + returned
    forces[...] = force
    residual = (force - target[...]) / atoms
    table[:, 0:atoms] = residual
    lent[...] = jnp.dot(residual, spots, precision=HIGHEST, preferred_element_type=F32)
    copies = [
        remote(lent, back.at[d], send.at[4 + d], recv.at[4 + d], below[d])
        for d in range(len(DIRECTIONS))
    ]
    for copy in copies:
        copy.wait()
    table[:, atoms:] = gathered(back)


def split(x):
    hi = x.astype(BF16)
    return hi, (x - hi.astype(F32)).astype(BF16)


def mm(a, b):
    return jnp.dot(a, b, preferred_element_type=F32)


def mm_t(a, b):
    return lax.dot_general(a, b, (((1,), (1,)), ((), ())), preferred_element_type=F32)


def round_up(n, k):
    return -(-n // k) * k


def onehot(ids, rows, cols):
    return jnp.where(lax.broadcasted_iota(jnp.int32, (rows, cols), 0) == ids, 1.0, 0.0).astype(BF16)


def slopes_of(z):
    sig = 0.5 * jnp.tanh(0.5 * z) + 0.5
    rest = 1.0 - sig
    act = z * sig
    d1 = sig + act * rest
    d2 = sig * rest * (2.0 + z * rest - act)
    return act, d1, d2


def phase_one(
    atoms,
    live, first, second, species, vec, table, w_a, w_b, w_radial, species_table, w_mid, w_out,
    ext, m1, mt, u_hi, u_lo, eg, zt, xs,
    c_hi, c_lo, wt_hi, wt_lo, w_hi, w_lo, wo, za, ta, md, eg_hi, eg_lo, wide,
):
    step = pl.program_id(0)
    extent, width = table.shape
    hidden = w_mid.shape[0]
    nb, ns = w_radial.shape[0], species_table.shape[0]
    pb = first.shape[1] // 2
    base = atoms + extent
    used = base + 2 * nb + ns

    @pl.when(step == 0)
    def _():
        wide[...] = jnp.zeros_like(wide)
        wide[0:atoms, :] = jnp.dot(table[0:atoms, :], w_a[...], precision=HIGHEST, preferred_element_type=F32)
        wide[atoms:base, :] = jnp.dot(table[...], w_b[...], precision=HIGHEST, preferred_element_type=F32)
        wide[base : base + nb, :] = w_radial[...]
        wide[base + nb : base + 2 * nb, :] = w_radial[...]
        wide[base + 2 * nb : used, :] = species_table[...]
        c_hi[...], c_lo[...] = split(wide[...].T)
        w_hi[...], w_lo[...] = split(w_mid[...])
        wt_hi[...], wt_lo[...] = split(w_mid[...].T)
        wo[...] = jnp.broadcast_to(w_out[...], (pb, hidden)).T
        ext[...] = jnp.zeros_like(ext)

    rows_at = [slice(i, i + hidden // 2) for i in range(0, hidden, hidden // 2)]
    chunks = [[slice(i, i + CHUNK) for i in range(r.start, r.stop, CHUNK)] for r in rows_at]
    slopes = [jnp.zeros((1, pb), F32), jnp.zeros((1, pb), F32)]

    def lanes_of(k):
        return slice(k * pb, (k + 1) * pb)

    def prepare(k):
        lane = lanes_of(k)
        square = jnp.sum(vec[:, lane] * vec[:, lane], axis=0, keepdims=True) + 1.0
        radius = jnp.sqrt(square)
        order = (lax.broadcasted_iota(jnp.int32, (nb, pb), 0) + 1).astype(F32) * (math.pi / RCUT)
        phase = order * radius
        sine, cosine = jnp.sin(phase), jnp.cos(phase)
        basis = sine / radius
        slope_basis = (order * cosine / radius - sine / square) / radius
        basis_hi = basis.astype(BF16).astype(F32)
        slope_hi = slope_basis.astype(BF16).astype(F32)
        m1[k, 0:atoms, :] = onehot(first[:, lane], atoms, pb)
        m1[k, atoms:base, :] = onehot(second[:, lane], extent, pb)
        m1[k, base : base + 2 * nb, :] = jnp.concatenate([basis_hi, basis - basis_hi], axis=0).astype(BF16)
        m1[k, base + 2 * nb : used, :] = onehot(species[:, lane], ns, pb)
        m1[k, used:, :] = jnp.zeros((m1.shape[1] - used, pb), BF16)
        mt[k, 0 : 2 * nb, :] = jnp.concatenate([slope_hi, slope_basis - slope_hi], axis=0).astype(BF16)
        mt[k, 2 * nb :, :] = jnp.zeros((mt.shape[1] - 2 * nb, pb), BF16)

    def first_dot(k, r):
        rows = rows_at[r]
        za[k, rows, :] = mm(c_hi[rows, :], m1[k]) + mm(c_lo[rows, :], m1[k])
        ta[k, rows, :] = mm(c_hi[rows, base:], mt[k]) + mm(c_lo[rows, base:], mt[k])

    def first_act(k, r):
        for rows in chunks[r]:
            z, t = za[k, rows, :], ta[k, rows, :]
            act, d1, d2 = slopes_of(z)
            za[k, rows, :] = d1
            ta[k, rows, :] = d2 * t
            u_hi[k, rows, 0:pb], u_lo[k, rows, 0:pb] = split(act)
            u_hi[k, rows, pb:], u_lo[k, rows, pb:] = split(d1 * t)

    def mid_dot(k, r):
        rows = rows_at[r]
        md[k, rows, :] = (
            mm(wt_hi[rows, :], u_hi[k]) + mm(wt_lo[rows, :], u_hi[k]) + mm(wt_hi[rows, :], u_lo[k])
        )

    def mid_act(k, r):
        for rows in chunks[r]:
            m, dm, out = md[k, rows, 0:pb], md[k, rows, pb:], wo[rows, :]
            _, d1, d2 = slopes_of(m)
            x = d1 * dm
            xs[k, rows, :] = x
            slopes[k] = slopes[k] + jnp.sum(out * x, axis=0, keepdims=True)
            e, g = out * d2 * dm, out * d1
            eg[k, rows, 0:pb] = e
            eg[k, rows, pb:] = g
            eg_hi[k, rows, 0:pb], eg_lo[k, rows, 0:pb] = split(e)
            eg_hi[k, rows, pb:], eg_lo[k, rows, pb:] = split(g)

    def back_dot(k, r):
        rows = rows_at[r]
        md[k, rows, :] = (
            mm(w_hi[rows, :], eg_hi[k]) + mm(w_lo[rows, :], eg_hi[k]) + mm(w_hi[rows, :], eg_lo[k])
        )

    def back_act(k, r):
        for rows in chunks[r]:
            e, g, d1 = md[k, rows, 0:pb], md[k, rows, pb:], za[k, rows, :]
            zt[k, rows, 0:pb] = e * d1 + g * ta[k, rows, :]
            zt[k, rows, pb:] = g * d1

    def push(k):
        slots = (step * 2 + k) * pb + lax.broadcasted_iota(jnp.int32, (1, pb), 1)
        coupling = jnp.where(slots < live[0, 0], slopes[k], 0.0)
        pushed = coupling * vec[:, lanes_of(k)]
        pushed_hi = pushed.astype(BF16).astype(F32)
        pushed2 = jnp.concatenate([pushed_hi, pushed - pushed_hi], axis=0).astype(BF16)
        half = pushed.shape[0]
        on_first = mm_t(pushed2, m1[k, 0:atoms, :])
        on_second = mm_t(pushed2, m1[k, atoms:base, :])
        ext[:, 0:atoms] += on_first[0:half] + on_first[half:]
        ext[...] -= on_second[0:half] + on_second[half:]

    prepare(0)
    prepare(1)
    first_dot(0, 0)
    first_dot(0, 1)
    for dot, dot_k, act, act_k in (
        (first_dot, 1, first_act, 0),
        (mid_dot, 0, first_act, 1),
        (mid_dot, 1, mid_act, 0),
        (back_dot, 0, mid_act, 1),
        (back_dot, 1, back_act, 0),
    ):
        for r in range(2):
            dot(dot_k, r)
            act(act_k, r)
    push(0)
    back_act(1, 0)
    back_act(1, 1)
    push(1)


def phase_two(
    atoms, nb, ns,
    live, first, vec, table, residual, m1, mt, u_hi, u_lo, eg, zt, xs,
    grads,
    we_hi, we_lo, zh, zl, th, tl, d_mid, d_wide, d_slope, d_out,
):
    step = pl.program_id(0)
    extent, width = table.shape
    hidden = u_hi.shape[1]
    pb = first.shape[1] // 2
    base = atoms + extent

    @pl.when(step == 0)
    def _():
        d_mid[...] = jnp.zeros_like(d_mid)
        d_wide[...] = jnp.zeros_like(d_wide)
        d_slope[...] = jnp.zeros_like(d_slope)
        d_out[...] = jnp.zeros_like(d_out)

    res = residual[...]
    res_hi = res.astype(BF16).astype(F32)
    res2 = jnp.concatenate([res_hi, res - res_hi], axis=0).astype(BF16)
    half = res.shape[0]

    def weigh(k):
        apart = mm(res2[:, 0:atoms], m1[k, 0:atoms, :]) - mm(res2, m1[k, atoms:base, :])
        slots = (step * 2 + k) * pb + lax.broadcasted_iota(jnp.int32, (1, pb), 1)
        moved = (apart[0:half] + apart[half:]) * vec[:, k * pb : (k + 1) * pb]
        return jnp.where(slots < live[0, 0], jnp.sum(moved, axis=0, keepdims=True), 0.0)

    def scale(k, r, weight):
        for i in range(r * hidden // 2, (r + 1) * hidden // 2, CHUNK):
            rows = slice(i, i + CHUNK)
            we_hi[k, rows, 0:pb], we_lo[k, rows, 0:pb] = split(eg[k, rows, 0:pb] * weight)
            we_hi[k, rows, pb:], we_lo[k, rows, pb:] = split(eg[k, rows, pb:] * weight)
            zh[k, rows, :], zl[k, rows, :] = split(zt[k, rows, 0:pb] * weight)
            th[k, rows, :], tl[k, rows, :] = split(zt[k, rows, pb:] * weight)
            x = xs[k, rows, :] * weight
            total = d_out[rows, :]
            for j in range(0, pb, LANES):
                total = total + x[:, j : j + LANES]
            d_out[rows, :] = total

    def contract(k, r):
        rows = slice(r * hidden // 2, (r + 1) * hidden // 2)
        d_mid[rows, :] += (
            mm_t(u_hi[k, rows, :], we_hi[k]) + mm_t(u_lo[k, rows, :], we_hi[k])
            + mm_t(u_hi[k, rows, :], we_lo[k])
        )
        rows = slice(r * m1.shape[1] // 2, (r + 1) * m1.shape[1] // 2)
        d_wide[rows, :] += mm_t(m1[k, rows, :], zh[k]) + mm_t(m1[k, rows, :], zl[k])

    def contract_slope(k):
        d_slope[...] += mm_t(mt[k, 0 : 2 * nb, :], th[k]) + mm_t(mt[k, 0 : 2 * nb, :], tl[k])

    weights = [weigh(0), weigh(1)]
    scale(0, 0, weights[0])
    scale(0, 1, weights[0])
    for r in range(2):
        contract(0, r)
        scale(1, r, weights[1])
    contract_slope(0)
    contract(1, 0)
    contract(1, 1)
    contract_slope(1)

    @pl.when(step == pl.num_programs(0) - 1)
    def _():
        across = table[...].T
        d_a = jnp.dot(across[:, 0:atoms], d_wide[0:atoms, :], precision=HIGHEST, preferred_element_type=F32)
        d_b = jnp.dot(across, d_wide[atoms:base, :], precision=HIGHEST, preferred_element_type=F32)
        d_radial = (
            d_wide[base : base + nb, :] + d_wide[base + nb : base + 2 * nb, :]
            + d_slope[0:nb, :] + d_slope[nb:, :]
        )
        d_species = d_wide[base + 2 * nb : base + 2 * nb + ns, :]
        d_last = jnp.broadcast_to(jnp.sum(d_out[...].T, axis=0, keepdims=True), (8, hidden))
        at = 0
        for piece in (d_a, d_b, d_mid[...], d_species, d_radial, d_last):
            n = piece.shape[0]
            for j in range(grads.shape[0]):
                grads[j, at : at + n, :] = piece[:, j * LANES : (j + 1) * LANES]
            at += n
        if at < grads.shape[1]:
            grads[:, at:, :] = jnp.zeros((grads.shape[0], grads.shape[1] - at, LANES), F32)


def unpack(packed, *outs):
    at = 0
    for out in outs:
        n = out.shape[0]
        for j in range(packed.shape[0]):
            out[:, j * LANES : (j + 1) * LANES] = packed[j, at : at + n, :]
        at += n


def sum_kernel(sizes, cut, mine, out, acc, from_core, in_a, in_b, in_c, in_d, in_z, send, recv):
    gc, gx, gy, gz = sizes
    bx, by = lax.axis_index("bx"), lax.axis_index("by")
    c, y = lax.rem(by, gc), lax.div(by, gc)
    x, z = lax.rem(bx, gx), lax.div(bx, gx)

    def place(px, pz, py, pc):
        return (pz * gx + px, py * gc + pc)

    def peers(me, size):
        return [(k, lax.rem(me + k, size)) for k in range(1, size)]

    cores = [(k, p, place(x, z, y, p)) for k, p in peers(c, gc)]
    xs = [(k, p, place(p, z, y, c)) for k, p in peers(x, gx)]
    ys = [(k, p, place(x, z, p, c)) for k, p in peers(y, gy)]
    zs = [(k, p, place(x, p, y, c)) for k, p in peers(z, gz)]
    everyone = cores + xs + ys + zs
    barrier = pltpu.get_barrier_semaphore()
    for _, _, device in everyone:
        pl.semaphore_signal(barrier, inc=1, device_id=device, device_id_type=MESH)
    pl.semaphore_wait(barrier, len(everyone))
    count = [0]

    def go(src, dst, device):
        slot = count[0]
        count[0] += 1
        copy = pltpu.make_async_remote_copy(
            src_ref=src, dst_ref=dst, send_sem=send.at[slot], recv_sem=recv.at[slot],
            device_id=device, device_id_type=MESH,
        )
        copy.start()
        return copy

    def finish(copies):
        for copy in copies:
            copy.wait()

    lower, upper = pl.ds(0, cut), pl.ds(cut, acc.shape[3] - cut)
    finish([go(mine.at[p], from_core.at[k - 1], d) for k, p, d in cores])
    total = mine[c]
    for k in range(gc - 1):
        total = total + from_core[k]
    acc[...] = total
    first = [go(acc.at[p, :, :, lower], in_a.at[k - 1], d) for k, p, d in xs]
    other = [go(acc.at[:, p, :, upper], in_b.at[k - 1], d) for k, p, d in ys]
    finish(first)
    for k in range(gx - 1):
        acc[x, :, :, lower] += in_a[k]
    first = [go(acc.at[x, p, :, lower], in_c.at[k - 1], d) for k, p, d in ys]
    finish(other)
    for k in range(gy - 1):
        acc[:, y, :, upper] += in_b[k]
    other = [go(acc.at[p, y, :, upper], in_d.at[k - 1], d) for k, p, d in xs]
    finish(first)
    for k in range(gy - 1):
        acc[x, y, :, lower] += in_c[k]
    finish(other)
    for k in range(gx - 1):
        acc[x, y, :, upper] += in_d[k]
    finish([go(acc.at[x, y, p], in_z.at[k - 1], d) for k, p, d in zs])
    total = acc[x, y, z]
    for k in range(gz - 1):
        total = total + in_z[k]
    out[c, x, y, z] = total
    finish([go(out.at[c, x, y, z], out.at[c, x, y, z], d) for k, p, d in zs])
    here = out.at[c, x, y, :, lower]
    first = [go(here, here, d) for k, p, d in ys]
    here = out.at[c, x, y, :, upper]
    other = [go(here, here, d) for k, p, d in xs]
    finish(first)
    here = out.at[c, x, :, :, lower]
    first = [go(here, here, d) for k, p, d in xs]
    finish(other)
    here = out.at[c, :, y, :, upper]
    other = [go(here, here, d) for k, p, d in ys]
    finish(first)
    finish(other)
    finish([go(out.at[c], out.at[c], d) for k, p, d in cores])


def sum_everywhere(packed, sizes, rows):
    gc, gx, gy, gz = sizes
    cut = (rows // 8 + 1) // 2 * 8
    n_copies = 2 * (gc - 1) + 4 * (gx - 1) + 4 * (gy - 1) + 2 * (gz - 1)
    shape = (gc, gx, gy, gz, rows, LANES)

    def room(*dims):
        return pltpu.VMEM(tuple(max(d, 1) for d in dims) + (LANES,), F32)

    whole = pl.BlockSpec(memory_space=pltpu.VMEM)
    return pl.pallas_call(
        functools.partial(sum_kernel, sizes, cut),
        out_shape=jax.ShapeDtypeStruct(shape, F32),
        in_specs=[whole],
        out_specs=whole,
        scratch_shapes=[
            room(gx, gy, gz, rows),
            room(gc - 1, gx, gy, gz, rows),
            room(gx - 1, gy, gz, cut),
            room(gy - 1, gx, gz, rows - cut),
            room(gy - 1, gz, cut),
            room(gx - 1, gz, rows - cut),
            room(gz - 1, rows),
            pltpu.SemaphoreType.DMA((n_copies,)),
            pltpu.SemaphoreType.DMA((n_copies,)),
        ],
        compiler_params=pltpu.CompilerParams(
            collective_id=1, has_side_effects=True, vmem_limit_bytes=VMEM_BYTES
        ),
        name="sum_grads",
    )(packed.reshape(shape))


def local(
    features,
    send_list,
    pair_first,
    pair_second,
    pair_species,
    pair_vector,
    live_pairs,
    force_target,
    w_a,
    w_b,
    w_radial,
    species_table,
    w_mid,
    w_out,
):
    local_feat = features[0, 0]
    sends = send_list[0, 0]
    first, second, species = pair_first[0], pair_second[0], pair_species[0]
    vec = jnp.pad(pair_vector[0, 0], ((0, 5), (0, 0)))
    target = force_target[0, 0]
    atoms, width = local_feat.shape
    ghosts = sends.shape[1]
    extent = atoms + 4 * ghosts
    hidden = w_mid.shape[0]
    nb, ns = w_radial.shape[0], species_table.shape[0]
    pairs = first.shape[1]
    pb = min(PBLOCK, pairs)
    steps = pairs // (2 * pb)
    deep = round_up(atoms + extent + 2 * nb + ns, LANES)
    thin = deep - atoms - extent

    sends = sends.reshape(1, 4 * ghosts)
    whole = pl.BlockSpec(memory_space=pltpu.VMEM)
    table = pl.pallas_call(
        fetch_rows,
        out_shape=jax.ShapeDtypeStruct((extent, width), F32),
        in_specs=[whole, whole],
        out_specs=whole,
        scratch_shapes=[
            pltpu.VMEM((4 * ghosts, width), F32),
            pltpu.SemaphoreType.DMA((4,)),
            pltpu.SemaphoreType.DMA((4,)),
        ],
        compiler_params=pltpu.CompilerParams(collective_id=2, has_side_effects=True),
        name="fetch_rows",
    )(local_feat, sends)

    smem = pl.BlockSpec(memory_space=pltpu.SMEM)

    def full(*dims):
        return pl.BlockSpec(dims, lambda i: (0,) * len(dims))

    def lane_block(rows):
        return pl.BlockSpec((rows, 2 * pb), lambda i: (0, i))

    def step_block(rows, cols):
        return pl.BlockSpec((2, rows, cols), lambda i: (i, 0, 0))

    def stacked(rows, cols, dtype):
        return jax.ShapeDtypeStruct((2 * steps, rows, cols), dtype)

    params = pltpu.CompilerParams(
        dimension_semantics=("arbitrary",), vmem_limit_bytes=VMEM_BYTES
    )
    kept_specs = [
        step_block(deep, pb),
        step_block(thin, pb),
        step_block(hidden, 2 * pb),
        step_block(hidden, 2 * pb),
        step_block(hidden, 2 * pb),
        step_block(hidden, 2 * pb),
        step_block(hidden, pb),
    ]
    ext, *kept = pl.pallas_call(
        functools.partial(phase_one, atoms),
        grid=(steps,),
        out_shape=[
            jax.ShapeDtypeStruct((8, extent), F32),
            stacked(deep, pb, BF16),
            stacked(thin, pb, BF16),
            stacked(hidden, 2 * pb, BF16),
            stacked(hidden, 2 * pb, BF16),
            stacked(hidden, 2 * pb, F32),
            stacked(hidden, 2 * pb, F32),
            stacked(hidden, pb, F32),
        ],
        in_specs=[
            smem,
            lane_block(1),
            lane_block(1),
            lane_block(1),
            lane_block(8),
            full(extent, width),
            full(width, hidden),
            full(width, hidden),
            full(nb, hidden),
            full(ns, hidden),
            full(hidden, hidden),
            full(1, hidden),
        ],
        out_specs=[full(8, extent)] + kept_specs,
        scratch_shapes=[
            pltpu.VMEM((hidden, deep), BF16),
            pltpu.VMEM((hidden, deep), BF16),
            pltpu.VMEM((hidden, hidden), BF16),
            pltpu.VMEM((hidden, hidden), BF16),
            pltpu.VMEM((hidden, hidden), BF16),
            pltpu.VMEM((hidden, hidden), BF16),
            pltpu.VMEM((hidden, pb), F32),
            pltpu.VMEM((2, hidden, pb), F32),
            pltpu.VMEM((2, hidden, pb), F32),
            pltpu.VMEM((2, hidden, 2 * pb), F32),
            pltpu.VMEM((2, hidden, 2 * pb), BF16),
            pltpu.VMEM((2, hidden, 2 * pb), BF16),
            pltpu.VMEM((deep, hidden), F32),
        ],
        compiler_params=params,
        name="edge_forward",
    )(
        live_pairs, first, second, species, vec, table, w_a, w_b, w_radial, species_table, w_mid,
        w_out[None],
    )
    forces, residual_table = pl.pallas_call(
        settle,
        out_shape=[
            jax.ShapeDtypeStruct((8, atoms), F32),
            jax.ShapeDtypeStruct((8, extent), F32),
        ],
        in_specs=[whole, whole, whole],
        out_specs=[whole, whole],
        scratch_shapes=[
            pltpu.VMEM((8, 4 * ghosts), F32),
            pltpu.VMEM((4, 8, 4 * ghosts), F32),
            pltpu.VMEM((8, 4 * ghosts), F32),
            pltpu.VMEM((4, 8, 4 * ghosts), F32),
            pltpu.SemaphoreType.DMA((8,)),
            pltpu.SemaphoreType.DMA((8,)),
        ],
        compiler_params=pltpu.CompilerParams(collective_id=3, has_side_effects=True),
        name="settle_forces",
    )(ext, sends, jnp.pad(target, ((0, 5), (0, 0))))

    nbx, nby = lax.axis_size("bx"), lax.axis_size("by")
    gx = 2 if nbx % 2 == 0 else 1
    gc = 2 if nby % 2 == 0 else 1
    sizes = (gc, gx, nby // gc, nbx // gx)
    devices = nbx * nby
    columns = hidden // LANES
    body = 2 * width + hidden + ns + nb + 8
    rows = round_up(-(-body * columns // devices), 8)
    while devices * rows % (8 * columns):
        rows += 8
    tall = devices * rows // columns
    packed = pl.pallas_call(
        functools.partial(phase_two, atoms, nb, ns),
        grid=(steps,),
        out_shape=jax.ShapeDtypeStruct((columns, tall, LANES), F32),
        in_specs=[smem, lane_block(1), lane_block(8), full(extent, width), full(8, extent)]
        + kept_specs,
        out_specs=full(columns, tall, LANES),
        scratch_shapes=[
            pltpu.VMEM((2, hidden, 2 * pb), BF16),
            pltpu.VMEM((2, hidden, 2 * pb), BF16),
            pltpu.VMEM((2, hidden, pb), BF16),
            pltpu.VMEM((2, hidden, pb), BF16),
            pltpu.VMEM((2, hidden, pb), BF16),
            pltpu.VMEM((2, hidden, pb), BF16),
            pltpu.VMEM((hidden, hidden), F32),
            pltpu.VMEM((deep, hidden), F32),
            pltpu.VMEM((2 * nb, hidden), F32),
            pltpu.VMEM((hidden, LANES), F32),
        ],
        compiler_params=params,
        name="edge_backward",
    )(live_pairs, first, vec, table, residual_table, *kept)
    summed = sum_everywhere(packed, sizes, rows).reshape(columns, tall, LANES)
    outs = pl.pallas_call(
        unpack,
        out_shape=[
            jax.ShapeDtypeStruct((n, hidden), F32) for n in (width, width, hidden, ns, nb, 8)
        ],
        compiler_params=pltpu.CompilerParams(vmem_limit_bytes=VMEM_BYTES),
        name="unpack_grads",
    )(summed)
    d_a, d_b, d_mid, d_species, d_radial, d_out = outs
    return (forces[None, None, 0:3], d_a, d_b, d_radial, d_species, d_mid, d_out[0])


def solution(mesh):
    return jax.shard_map(
        local,
        mesh=mesh,
        in_specs=(
            P("bx", "by", None, None),
            P("bx", "by", None, None),
            P("bx", "by", None),
            P("bx", "by", None),
            P("bx", "by", None),
            P("bx", "by", None, None),
            P("bx", "by"),
            P("bx", "by", None, None),
            P(),
            P(),
            P(),
            P(),
            P(),
            P(),
        ),
        out_specs=(P("bx", "by", None, None), P(), P(), P(), P(), P(), P()),
        check_vma=False,
    )
```
